32 devices in a mesh: grp: 2 (over y), src: 4 (over z), rcv: 2 (over x), tim: 2 (over core).
Axes of the slice: x: 2, y: 2, z: 4, core: 2. Of those that a mesh axis runs over, the one named last changes fastest.
Arguments:
- response: bfloat16 [2048, 128, 2048], P('src', 'tim', 'rcv'), may hold values from -80 to 80, as said below
- onset: int32 [2048, 2048], P('src', 'rcv'), may hold values from 0 to 127
- direct_wave: bfloat16 [4096, 256], P(('grp', 'rcv'), 'src'), parts along dimension 0, may hold values from -6 to 6
- arrival: int32 [4096], P('grp'), parts along dimension 0, may hold values from 64 to 255
Outputs:
- focus_down: bfloat16 [4096, 256], P(('grp', 'rcv'), 'src'), parts along dimension 0
- focus_up: bfloat16 [4096, 256], P(('grp', 'src')), parts along dimension 0
The draws below stay inside these ranges and needn't reach their ends.
There are 2 independent parts, one for each index of `grp`. The reference program is written for one: setup_inputs(seed, part) draws one part's arguments, and reference() takes and returns one part's arrays. A program takes and returns all parts, laid end to end along the dimension named above; an argument that names none is the same for every part. Nothing has to cross between parts.
Inputs may be any that keep to these rules, and one draw needn't show every extreme that they name: response is a reflection response in the printed table's range.
All inputs are finite; a program needn't handle non-finite values.
Results may differ from the reference program's by a relative error of at most 0.015.
Values may be sent and summed in bfloat16 or wider, within the bound.
No kernel may reach another device: no remote copies, remote signals or barrier semaphores. Data moves between devices by JAX's collectives and lax.ppermute only.
A program may use at most 320 MiB of HBM per device.

```python
import math
import jax
import jax.numpy as jnp
from jax import lax

STATIONS = 2048
TAPS = 128
TIME = 256
ITERS = 2


def draw_response(key, part):
    subkeys = jax.random.split(jax.random.fold_in(key, 17), 4)
    position = (jnp.arange(STATIONS, dtype=jnp.float32) + 0.5) / STATIONS
    tap_level = jnp.arange(TAPS, dtype=jnp.float32) / TAPS
    samples = jnp.clip(jax.random.normal(subkeys[0], (STATIONS, TAPS, STATIONS), jnp.float32), -6.0, 6.0)
    src_trend = position
    tap_envelope = jnp.power(3.0, -tap_level)
    src_scale = jnp.power(10.0, src_trend + jax.random.uniform(subkeys[2], (STATIONS,), jnp.float32, -0.05, 0.05))
    rcv_scale = jnp.power(10.0, position + jax.random.uniform(subkeys[3], (STATIONS,), jnp.float32, -0.05, 0.05))
    return (0.1 * samples * src_scale[:, None, None] * tap_envelope[None, :, None] * rcv_scale[None, None, :]).astype(jnp.bfloat16)


def touch_ends(result, own_key, least, top_value):
    longest = result.shape.index(max(result.shape))
    spots = []
    for shift in (0, 1):
        where = [jax.random.randint(jax.random.fold_in(own_key, axis), (), 0, length) for axis, length in enumerate(result.shape)]
        where[longest] = (where[longest] + shift) % result.shape[longest]
        spots.append(tuple(where))
    return result.at[spots[0]].set(least).at[spots[1]].set(top_value)


def block_scale(stream_key, dims, shards, smallest, top_value):
    level, own = 1.0, jax.random.fold_in(stream_key, 6)
    for dim, parts in shards:
        steps = jnp.exp(jax.random.uniform(jax.random.fold_in(own, dim), (parts,), jnp.float32, smallest / len(shards), top_value / len(shards)))
        level = level * jnp.repeat(steps, dims[dim] // parts).reshape([-1 if axis == dim else 1 for axis in range(len(dims))])
    return level


def gaussian(key, shape, width, most, cuts=(), kind=jnp.bfloat16):
    array = width * jax.random.normal(key, shape, jnp.float32)
    if cuts:
        array = array * block_scale(key, shape, cuts, -0.22, 0.18)
    return jnp.clip(array, -most, most).astype(kind)


def setup_inputs(seed: int = 0, part: int = 0) -> dict:
    key_list = jax.random.split(jax.random.key(seed), 5)
    part_splits = jax.random.split(jax.random.fold_in(key_list[4], part), 5)
    response = draw_response(jax.random.fold_in(key_list[4], 71), part)
    onset = touch_ends(jax.random.randint(key_list[1], (STATIONS, STATIONS), 0, TAPS), jax.random.fold_in(key_list[1], 1), 0, TAPS - 1).astype(jnp.int32)
    direct_wave = gaussian(part_splits[2], (STATIONS, TIME), 1.0, 6.0, ((0, 2), (1, 4)))
    arrival = touch_ends(jax.random.randint(part_splits[3], (STATIONS,), TIME // 4, TIME), jax.random.fold_in(part_splits[3], 1), TIME // 4, TIME - 1).astype(jnp.int32)
    return {"response": response, "onset": onset, "direct_wave": direct_wave, "arrival": arrival}


def delay_sum(product, offset):
    row_count, taps_here, time_span = product.shape
    row_width = time_span + taps_here
    padded = jnp.pad(product, ((0, 0), (0, 0), (0, taps_here)))
    flattened = padded.reshape(row_count, taps_here * row_width)[:, :taps_here * (row_width - 1)]
    sheared = flattened.reshape(row_count, taps_here, row_width - 1)
    summed = lax.optimization_barrier(jnp.sum(sheared, axis=1))[:, :time_span]
    framed = jnp.concatenate([jnp.zeros((row_count, time_span), jnp.float32), summed], axis=1)
    return lax.dynamic_slice_in_dim(framed, time_span - offset, time_span, 1)

def advance_stack(series, taps_here, offset):
    row_count, time_span = series.shape
    framed = jnp.concatenate([series, jnp.zeros((row_count, time_span), series.dtype)], axis=1)
    row_width = time_span + taps_here
    advanced = lax.dynamic_slice_in_dim(framed, offset, row_width, 1)
    repeated = jnp.broadcast_to(advanced[:, None, :], (row_count, taps_here, row_width))
    repeated = repeated.reshape(row_count, taps_here * row_width)
    repeated = jnp.pad(repeated, ((0, 0), (0, taps_here)))
    return repeated.reshape(row_count, taps_here, row_width + 1)[:, :, :time_span]

def reference(response, onset, direct_wave, arrival):
    block_rows = math.gcd(STATIONS, 128)
    block_count = STATIONS // block_rows
    resp_blocks = response.reshape(block_count, block_rows, TAPS, STATIONS)
    onset_blocks = onset.reshape(block_count, block_rows, STATIONS)
    tap_index = lax.broadcasted_iota(jnp.int32, (1, TAPS, 1), 1)
    time_index = lax.broadcasted_iota(jnp.int32, (1, TIME), 1)

    def energy_step(accumulated, resp_block):
        return (accumulated + jnp.sum(jnp.square(resp_block.astype(jnp.float32))), None)
    energy, _ = lax.scan(energy_step, jnp.zeros((), jnp.float32), resp_blocks)
    unit_gain = lax.rsqrt(energy / STATIONS + 1e-06)

    def masked(resp_block, starts):
        kept_resp = jnp.where(tap_index >= starts[:, None, :], resp_block, jnp.zeros((), resp_block.dtype))
        return kept_resp.astype(jnp.float32).reshape(block_rows * TAPS, STATIONS)
    field = direct_wave
    focus_up = direct_wave
    for iteration in range(ITERS):
        field_wide = field.astype(jnp.float32)

        def forward(operands):
            resp_block, starts = operands
            product = jnp.dot(masked(resp_block, starts), field_wide, preferred_element_type=jnp.float32)
            return delay_sum(product.reshape(block_rows, TAPS, TIME), 0)
        forward_sum = lax.map(forward, (resp_blocks, onset_blocks)).reshape(STATIONS, TIME)
        focus_up = jnp.where(time_index < arrival[:, None], unit_gain * forward_sum, 0.0).astype(jnp.bfloat16)
        up_blocks = focus_up.reshape(block_count, block_rows, TIME)

        def backward(accumulated, operands):
            resp_block, starts, up_block = operands
            stacked = advance_stack(up_block, TAPS, 0).astype(jnp.float32).reshape(block_rows * TAPS, TIME)
            return (accumulated + jnp.dot(masked(resp_block, starts).T, stacked, preferred_element_type=jnp.float32), None)
        backward_sum, _ = lax.scan(backward, jnp.zeros((STATIONS, TIME), jnp.float32), (resp_blocks, onset_blocks, up_blocks))
        field = (direct_wave.astype(jnp.float32) + jnp.where(time_index < arrival[:, None], unit_gain * backward_sum, 0.0)).astype(jnp.bfloat16)
    return (field, focus_up)
```

```python
import functools

import jax
import jax.numpy as jnp
from jax import lax
from jax.experimental import pallas as pl
from jax.experimental.pallas import tpu as pltpu
from jax.sharding import PartitionSpec as P

STATIONS = 2048
ITERS = 2
MIB = 1 << 20
bf16 = jnp.bfloat16
f32 = jnp.float32
VM = pl.BlockSpec(memory_space=pltpu.VMEM)
SM = pl.BlockSpec(memory_space=pltpu.SMEM)
ANY = pl.BlockSpec(memory_space=pl.ANY)


def load_kernel(pos_ref, r_hbm, on_hbm, k_ref, e_out, on_ref, e_ref, sem, *, chunks, sub):
    rows, taps, cols = k_ref.shape
    size = rows // chunks
    start = pl.multiple_of(pos_ref[0], 8)
    tap_start = pos_ref[1]

    def part(c):
        return pltpu.make_async_copy(
            r_hbm.at[pl.ds(start + c * size, size)], k_ref.at[pl.ds(c * size, size)], sem.at[c]
        )

    onset_copy = pltpu.make_async_copy(on_hbm.at[pl.ds(start, rows)], on_ref, sem.at[chunks])
    onset_copy.start()
    for c in range(chunks):
        part(c).start()
    e_ref[...] = jnp.zeros_like(e_ref)
    tap = lax.broadcasted_iota(jnp.int32, (1, taps, 1), 1).astype(f32).astype(bf16)
    onset_copy.wait()
    for c in range(chunks):
        part(c).wait()

        def body(b, carry):
            at = pl.multiple_of(c * size + b * sub, sub)
            r = k_ref[pl.ds(at, sub)]
            x = r.astype(f32)
            e_ref[...] += jnp.sum((x * x).reshape(sub * taps // 8, 8, cols), axis=0)
            on = (on_ref[pl.ds(at, sub)] - tap_start).astype(f32).astype(bf16)
            keep = jnp.broadcast_to(tap, r.shape) >= on[:, None, :]
            k_ref[pl.ds(at, sub)] = jnp.where(keep, r, jnp.zeros((), bf16))
            return carry

        lax.fori_loop(0, size // sub, body, 0)
    e_out[0] = jnp.sum(e_ref[...])


def load_kept(pos, response, onset, rows):
    _, taps, cols = response.shape
    sub = 8
    chunks = max(1, min(16, rows // sub))
    return pl.pallas_call(
        functools.partial(load_kernel, chunks=chunks, sub=sub),
        in_specs=[SM, ANY, ANY],
        out_specs=[VM, SM],
        out_shape=[pltpu.VMEM((rows, taps, cols), bf16), jax.ShapeDtypeStruct((1,), f32)],
        scratch_shapes=[
            pltpu.VMEM((rows, cols), jnp.int32),
            pltpu.VMEM((8, cols), f32),
            pltpu.SemaphoreType.DMA((chunks + 1,)),
        ],
        compiler_params=pltpu.CompilerParams(vmem_limit_bytes=14 * MIB),
        cost_estimate=pl.CostEstimate(
            flops=0, bytes_accessed=rows * taps * cols * 2, transcendentals=0
        ),
        name="load_kept",
    )(pos, response, onset)


def steps_of(rows):
    sub = min(16, rows)
    unroll = 2 if rows % (2 * sub) == 0 else 1
    return sub, unroll


def forward_kernel(pos_ref, k_ref, f_ref, o_ref, *, first, groups):
    taps, cols = k_ref.shape[1:]
    rows = o_ref.shape[0]
    time = f_ref.shape[0] // groups
    sub, unroll = steps_of(rows)
    tap_start = pos_ref[1]
    sample = lax.broadcasted_iota(jnp.int32, (8, time), 0) + lax.broadcasted_iota(
        jnp.int32, (8, time), 1
    )

    def body(step, carry):
        for u in range(unroll):
            at = pl.multiple_of((step * unroll + u) * sub, sub)
            k = k_ref[pl.ds(first + at, sub)].reshape(sub * taps, cols)
            p = lax.dot_general(
                k, f_ref[...], (((1,), (1,)), ((), ())), preferred_element_type=f32
            )
            p = p.reshape(sub, taps // 8, 8, groups * time)
            for g in range(groups):
                total = None
                for j in range(taps // 8 - 1, -1, -1):
                    inside = (sample < time - tap_start - 8 * j)[None]
                    term = jnp.where(inside, p[:, j, :, g * time : (g + 1) * time], 0.0)
                    total = term if total is None else pltpu.roll(total, 8, 2) + term
                total = pltpu.roll(total, 0, 2, stride=1, stride_axis=1)
                o_ref[pl.ds(at, sub), g * time : (g + 1) * time] = pltpu.roll(
                    jnp.sum(total, axis=1), tap_start, 1
                )
        return carry

    lax.fori_loop(0, rows // (sub * unroll), body, 0)


def forward(pos, kept, field, first, rows, groups):
    _, taps, cols = kept.shape
    width = field.shape[0]
    return pl.pallas_call(
        functools.partial(forward_kernel, first=first, groups=groups),
        in_specs=[SM, VM, VM],
        out_specs=VM,
        out_shape=jax.ShapeDtypeStruct((rows, width), f32),
        compiler_params=pltpu.CompilerParams(vmem_limit_bytes=24 * MIB),
        cost_estimate=pl.CostEstimate(
            flops=2 * rows * taps * cols * width, bytes_accessed=width * cols * 2, transcendentals=0
        ),
        name="forward",
    )(pos, pltpu.with_memory_space_constraint(kept, pltpu.VMEM), field)


def backward_kernel(pos_ref, k_ref, u_ref, *refs, first, groups):
    before_ref, (o_ref, acc_ref) = (refs[0] if len(refs) == 3 else None), refs[-2:]
    taps, cols = k_ref.shape[1:]
    rows = u_ref.shape[0]
    time = u_ref.shape[1] // groups
    sub, unroll = steps_of(rows)
    tap_start = pos_ref[1]
    sample = lax.broadcasted_iota(jnp.int32, (8, time), 0) + lax.broadcasted_iota(
        jnp.int32, (8, time), 1
    )
    acc_ref[...] = jnp.zeros_like(acc_ref) if before_ref is None else before_ref[...]

    def body(step, carry):
        for n in range(unroll):
            at = pl.multiple_of((step * unroll + n) * sub, sub)
            k = k_ref[pl.ds(first + at, sub)].reshape(sub * taps, cols)
            stacks = []
            for g in range(groups):
                u = u_ref[pl.ds(at, sub), g * time : (g + 1) * time].astype(f32)
                u = pltpu.roll(u, time - tap_start, 1)
                base = jnp.stack([pltpu.roll(u, time - i, 1) if i else u for i in range(8)], axis=1)
                terms = []
                for j in range(taps // 8):
                    moved = pltpu.roll(base, time - 8 * j, 2) if j else base
                    inside = (sample < time - tap_start - 8 * j)[None]
                    terms.append(jnp.where(inside, moved, 0.0))
                stacks.append(jnp.stack(terms, 1).astype(bf16).reshape(sub * taps, time))
            stacked = jnp.concatenate(stacks, axis=1)
            acc_ref[...] += lax.dot_general(
                stacked, k, (((0,), (0,)), ((), ())), preferred_element_type=f32
            )
        return carry

    lax.fori_loop(0, rows // (sub * unroll), body, 0)
    o_ref[...] = acc_ref[...].astype(o_ref.dtype)


def backward(pos, kept, up, before, first, groups, kind):
    _, taps, cols = kept.shape
    rows, width = up.shape
    more = [] if before is None else [before]
    return pl.pallas_call(
        functools.partial(backward_kernel, first=first, groups=groups),
        in_specs=[SM, VM, VM] + [VM] * len(more),
        out_specs=VM,
        out_shape=jax.ShapeDtypeStruct((width, cols), kind),
        scratch_shapes=[pltpu.VMEM((width, cols), f32)],
        compiler_params=pltpu.CompilerParams(vmem_limit_bytes=24 * MIB),
        cost_estimate=pl.CostEstimate(
            flops=2 * rows * taps * cols * width, bytes_accessed=width * cols * 4, transcendentals=0
        ),
        name="backward",
    )(pos, pltpu.with_memory_space_constraint(kept, pltpu.VMEM), up, *more)


def shifted(x, axis, shift):
    n = lax.axis_size(axis)
    return lax.ppermute(x, axis, [(i, (i + shift) % n) for i in range(n)])


def gather(x, axis):
    n = lax.axis_size(axis)
    if n == 1:
        return x[None]
    if n > 8:
        return lax.all_gather(x, axis)
    got = [x] + [shifted(x, axis, -k) for k in range(1, n)]
    ring = jnp.stack(got + got[:-1])
    return lax.dynamic_slice_in_dim(ring, (n - lax.axis_index(axis)) % n, n, 0)


def scatter_parts(x, axis):
    n = lax.axis_size(axis)
    me = lax.axis_index(axis)
    if n == 1:
        return [x[0]]
    if n > 8:
        got = lax.all_to_all(x, axis, 0, 0, tiled=True)
        return [got[i] for i in range(n)]
    parts = [lax.dynamic_index_in_dim(x, me, 0, False)]
    for k in range(1, n):
        parts.append(shifted(lax.dynamic_index_in_dim(x, (me + k) % n, 0, False), axis, k))
    return parts


def total_of(parts):
    total = parts[0].astype(f32)
    for part in parts[1:]:
        total = total + part.astype(f32)
    return total


def on_device(response, onset, direct_wave, arrival):
    src_rows, tap_rows, rcv_rows = response.shape
    tile_time = direct_wave.shape[1]
    groups, src_n, tim_n = (lax.axis_size(a) for a in ("grp", "src", "tim"))
    g, s, r, c = (lax.axis_index(a) for a in ("grp", "src", "rcv", "tim"))
    time = src_n * tile_time
    rows = src_rows // groups
    part_time = tile_time // tim_n
    pos = jnp.stack([g * rows, c * tap_rows]).astype(jnp.int32)

    direct_piece = lax.dynamic_slice_in_dim(direct_wave, c * part_time, part_time, 1).T
    my_arrival = lax.dynamic_slice_in_dim(arrival, s * src_rows, src_rows).reshape(groups, rows)
    src_arrival = jnp.stack(total_order(scatter_parts(my_arrival, "grp"), "grp"))
    rcv_arrival = lax.dynamic_slice_in_dim(arrival, r * rcv_rows, rcv_rows)

    def whole_field(piece):
        field = gather(gather(gather(piece, "grp"), "src"), "tim")
        return field.transpose(2, 1, 0, 3, 4).reshape(groups * time, rcv_rows)

    current = whole_field(direct_piece)
    kept, energy = load_kept(pos, response, onset, rows)
    energy = jnp.broadcast_to(energy, (8, 128))
    for axis in ("tim", "rcv", "grp", "src"):
        energy = jnp.sum(gather(energy, axis), axis=0)
    unit_gain = lax.rsqrt(energy[0, 0] / STATIONS + 1e-06)

    halves = 2 if rows % 32 == 0 and rows >= 64 else 1
    half = rows // halves
    share = half // tim_n
    up_time = lax.broadcasted_iota(jnp.int32, (1, 1, time), 2)
    piece_time = s * tile_time + c * part_time
    piece_time = piece_time + lax.broadcasted_iota(jnp.int32, (part_time, 1), 0)

    focus_up = piece = None
    for iteration in range(ITERS):
        final_pass = iteration + 1 == ITERS
        ups, outs = [], []
        for h in range(halves):
            partial = forward(pos, kept, current, h * half, half, groups)
            partial = partial.astype(bf16).reshape(tim_n, share, groups * time)
            mine = total_of(scatter_parts(partial, "tim")).astype(bf16)
            total = jnp.sum(gather(mine, "rcv").astype(f32), axis=0)
            total = total.reshape(share, groups, time)
            limit = lax.dynamic_slice_in_dim(src_arrival, h * half + c * share, share, 1)
            inside = up_time < limit.T[:, :, None]
            up = jnp.where(inside, total, 0.0).reshape(share, groups * time)
            ups.append(gather(up.astype(bf16), "tim").reshape(half, groups * time))
            if final_pass:
                scaled = jnp.where(inside, unit_gain * total, 0.0).astype(bf16)
                outs.append(gather(scaled, "tim").reshape(half, groups, time))
        acc = None
        for h in range(halves):
            kind = bf16 if h + 1 == halves else f32
            acc = backward(pos, kept, ups[h], acc, h * half, groups, kind)
        sums = acc.reshape(groups, src_n, tim_n, part_time, rcv_rows)
        sums = total_of(scatter_parts(sums.transpose(2, 0, 1, 3, 4), "tim")).astype(bf16)
        sums = total_of(scatter_parts(sums, "grp")).astype(bf16)
        sums = total_of(scatter_parts(sums, "src"))
        piece = (
            direct_piece.astype(f32)
            + jnp.where(piece_time < rcv_arrival[None, :], unit_gain * unit_gain * sums, 0.0)
        ).astype(bf16)
        if final_pass:
            out = jnp.concatenate(outs).transpose(1, 0, 2)
            focus_up = jnp.concatenate(total_order(scatter_parts(out, "grp"), "grp"))
            focus_down = gather(piece, "tim").reshape(tile_time, rcv_rows).T
        else:
            current = whole_field(piece)
    return (focus_down, focus_up)


def total_order(parts, axis):
    n = lax.axis_size(axis)
    if n == 1 or n > 8:
        return parts
    stack = jnp.stack(parts)
    me = lax.axis_index(axis)
    return [lax.dynamic_index_in_dim(stack, (me - i) % n, 0, False) for i in range(n)]


def solution(mesh):
    in_specs = (P("src", "tim", "rcv"), P("src", "rcv"), P(("grp", "rcv"), "src"), P("grp"))
    out_specs = (P(("grp", "rcv"), "src"), P(("grp", "src"), None))
    return jax.shard_map(
        on_device, mesh=mesh, in_specs=in_specs, out_specs=out_specs, check_vma=False
    )
```

```python
import functools

import jax
import jax.numpy as jnp
from jax import lax
from jax.experimental import pallas as pl
from jax.experimental.pallas import tpu as pltpu
from jax.sharding import PartitionSpec as P

STATIONS = 2048
ITERS = 2
MIB = 1 << 20
bf16 = jnp.bfloat16
f32 = jnp.float32
VM = pl.BlockSpec(memory_space=pltpu.VMEM)
SM = pl.BlockSpec(memory_space=pltpu.SMEM)
ANY = pl.BlockSpec(memory_space=pl.ANY)


class Stream:
    def __init__(self, k_hbm, ring, sem, size):
        self.k_hbm, self.ring, self.sem, self.size = k_hbm, ring, sem, size
        self.slots, self.count = ring.shape[0], k_hbm.shape[0] // size

    def copy(self, step):
        slot = lax.rem(step, self.slots)
        return pltpu.make_async_copy(
            self.k_hbm.at[pl.ds(step * self.size, self.size)], self.ring.at[slot], self.sem.at[slot]
        )

    def start(self):
        for c in range(min(self.slots - 1, self.count)):
            self.copy(jnp.int32(c)).start()

    def next(self, step):
        self.copy(step).wait()

        @pl.when(step + self.slots - 1 < self.count)
        def _():
            self.copy(step + self.slots - 1).start()

        return lax.rem(step, self.slots)


def ring_of(rows, taps, cols):
    sub, unroll = steps_of(rows)
    return [pltpu.VMEM((3, sub * unroll, taps, cols), bf16), pltpu.SemaphoreType.DMA((3,))]


def steps_of(rows):
    sub = min(16, rows)
    unroll = 2 if rows % (2 * sub) == 0 else 1
    return sub, unroll


def place_blocks(where_ref, blocks, f_ref):
    many, size = blocks[0].shape[0], blocks[0].shape[1]
    for b, block in enumerate(blocks):
        for i in range(many):
            to = where_ref[b * many + i]
            f_ref[pl.ds(pl.multiple_of(to, size), size)] = block[i]


def shear_sum(k, f_ref, tap_start, groups, put):
    sub, taps, cols = k.shape
    time = f_ref.shape[0] // groups
    sample = lax.broadcasted_iota(jnp.int32, (8, time), 0) + lax.broadcasted_iota(
        jnp.int32, (8, time), 1
    )
    p = lax.dot_general(
        k.reshape(sub * taps, cols),
        f_ref[...],
        (((1,), (1,)), ((), ())),
        preferred_element_type=f32,
    )
    p = p.reshape(sub, taps // 8, 8, groups * time)
    for g in range(groups):
        total = None
        for j in range(taps // 8 - 1, -1, -1):
            inside = (sample < time - tap_start - 8 * j)[None]
            term = jnp.where(inside, p[:, j, :, g * time : (g + 1) * time], 0.0)
            total = term if total is None else pltpu.roll(total, 8, 2) + term
        total = pltpu.roll(total, 0, 2, stride=1, stride_axis=1)
        put(g * time, (g + 1) * time, pltpu.roll(jnp.sum(total, axis=1), tap_start, 1))


def forward_kernel(pos_ref, where_ref, k_hbm, *refs, groups, waits):
    blocks, (o_ref, f_ref, ring, sem) = refs[waits:-4], refs[-4:]
    rows, taps, cols = k_hbm.shape
    sub, unroll = steps_of(rows)
    stream = Stream(k_hbm, ring, sem, sub * unroll)
    stream.start()
    tap_start = pos_ref[1]
    place_blocks(where_ref, blocks, f_ref)

    def body(step, carry):
        slot = stream.next(step)
        for u in range(unroll):
            at = pl.multiple_of((step * unroll + u) * sub, sub)

            def put(lo, hi, value):
                o_ref[pl.ds(at, sub), lo:hi] = value

            k = ring[slot, u * sub : (u + 1) * sub]
            shear_sum(k, f_ref, tap_start, groups, put)
        return carry

    lax.fori_loop(0, rows // (sub * unroll), body, 0)


def first_kernel(pos_ref, where_ref, r_hbm, on_hbm, *refs, groups, waits):
    blocks, refs = refs[waits:-10], refs[-10:]
    o_ref, k_hbm, e_out, f_ref, ring, sem, out_sem, on_ref, e_ref, on_sem = refs
    rows, taps, cols = k_hbm.shape
    sub, unroll = steps_of(rows)
    size, slots = sub * unroll, ring.shape[0]
    count = rows // size
    ahead = slots - 2
    start = pl.multiple_of(pos_ref[0], 8)
    tap_start = pos_ref[1]

    def part(step):
        slot = lax.rem(step, slots)
        return pltpu.make_async_copy(
            r_hbm.at[pl.ds(start + step * size, size)], ring.at[slot], sem.at[slot]
        )

    def result(step):
        slot = lax.rem(step, slots)
        return pltpu.make_async_copy(
            ring.at[slot], k_hbm.at[pl.ds(step * size, size)], out_sem.at[slot]
        )

    onset_copy = pltpu.make_async_copy(on_hbm.at[pl.ds(start, rows)], on_ref, on_sem)
    onset_copy.start()
    for n in range(min(ahead, count)):
        part(jnp.int32(n)).start()
    e_ref[...] = jnp.zeros_like(e_ref)
    tap = lax.broadcasted_iota(jnp.int32, (1, taps, 1), 1).astype(f32).astype(bf16)
    place_blocks(where_ref, blocks, f_ref)
    onset_copy.wait()

    def body(step, carry):
        slot = lax.rem(step, slots)
        part(step).wait()

        @pl.when(step + ahead < count)
        def _():
            @pl.when(step >= slots - ahead)
            def _():
                result(step - (slots - ahead)).wait()

            part(step + ahead).start()

        for u in range(unroll):
            at = pl.multiple_of((step * unroll + u) * sub, sub)

            def put(lo, hi, value):
                o_ref[pl.ds(at, sub), lo:hi] = value

            for v in range(0, sub, 8):
                r = ring[slot, u * sub + v : u * sub + v + 8]
                x = r.astype(f32)
                e_ref[...] += jnp.sum((x * x).reshape(taps, 8, cols), axis=0)
                on = (on_ref[pl.ds(at + v, 8)] - tap_start).astype(f32).astype(bf16)
                keep = jnp.broadcast_to(tap, r.shape) >= on[:, None, :]
                ring[slot, u * sub + v : u * sub + v + 8] = jnp.where(keep, r, jnp.zeros((), bf16))
            k = ring[slot, u * sub : (u + 1) * sub]
            shear_sum(k, f_ref, tap_start, groups, put)
        result(step).start()
        return carry

    lax.fori_loop(0, count, body, 0)
    for n in range(max(0, count - slots), count):
        result(jnp.int32(n)).wait()
    e_out[0] = jnp.sum(e_ref[...])


def first_forward(pos, where, response, onset, blocks, rows, width, after):
    _, taps, cols = response.shape
    groups = lax.axis_size("grp")
    sub, unroll = steps_of(rows)
    slots = 4
    return pl.pallas_call(
        functools.partial(first_kernel, groups=groups, waits=len(after)),
        in_specs=[SM, SM, ANY, ANY] + [ANY] * len(after) + [VM] * len(blocks),
        out_specs=[VM, ANY, SM],
        out_shape=[
            jax.ShapeDtypeStruct((rows, width), f32),
            pltpu.HBM((rows, taps, cols), bf16),
            jax.ShapeDtypeStruct((1,), f32),
        ],
        scratch_shapes=[
            pltpu.VMEM((width, cols), bf16),
            pltpu.VMEM((slots, sub * unroll, taps, cols), bf16),
            pltpu.SemaphoreType.DMA((slots,)),
            pltpu.SemaphoreType.DMA((slots,)),
            pltpu.VMEM((rows, cols), jnp.int32),
            pltpu.VMEM((8, cols), f32),
            pltpu.SemaphoreType.DMA,
        ],
        compiler_params=pltpu.CompilerParams(vmem_limit_bytes=44 * MIB),
        cost_estimate=pl.CostEstimate(
            flops=2 * rows * taps * cols * width, bytes_accessed=width * cols * 2, transcendentals=0
        ),
        name="first_forward",
    )(pos, where, response, onset, *after, *blocks)


def forward(pos, where, kept, blocks, width, after):
    rows, taps, cols = kept.shape
    groups = lax.axis_size("grp")
    return pl.pallas_call(
        functools.partial(forward_kernel, groups=groups, waits=len(after)),
        in_specs=[SM, SM, ANY] + [ANY] * len(after) + [VM] * len(blocks),
        out_specs=VM,
        out_shape=jax.ShapeDtypeStruct((rows, width), f32),
        scratch_shapes=[pltpu.VMEM((width, cols), bf16)] + ring_of(rows, taps, cols),
        compiler_params=pltpu.CompilerParams(vmem_limit_bytes=40 * MIB),
        cost_estimate=pl.CostEstimate(
            flops=2 * rows * taps * cols * width, bytes_accessed=width * cols * 2, transcendentals=0
        ),
        name="forward",
    )(pos, where, pltpu.with_memory_space_constraint(kept, pltpu.HBM), *after, *blocks)


def backward_kernel(pos_ref, k_hbm, u_ref, *refs, groups, waits):
    refs = refs[waits:]
    before_ref, (o_ref, acc_ref, ring, sem) = (refs[0] if len(refs) == 5 else None), refs[-4:]
    rows, taps, cols = k_hbm.shape
    sub, unroll = steps_of(rows)
    stream = Stream(k_hbm, ring, sem, sub * unroll)
    stream.start()
    time = u_ref.shape[1] // groups
    tap_start = pos_ref[1]
    sample = lax.broadcasted_iota(jnp.int32, (8, time), 0) + lax.broadcasted_iota(
        jnp.int32, (8, time), 1
    )
    acc_ref[...] = jnp.zeros_like(acc_ref) if before_ref is None else before_ref[...]

    def body(step, carry):
        slot = stream.next(step)
        for n in range(unroll):
            at = pl.multiple_of((step * unroll + n) * sub, sub)
            k = ring[slot, n * sub : (n + 1) * sub].reshape(sub * taps, cols)
            stacks = []
            for g in range(groups):
                u = u_ref[pl.ds(at, sub), g * time : (g + 1) * time].astype(f32)
                u = pltpu.roll(u, time - tap_start, 1)
                base = jnp.stack([pltpu.roll(u, time - i, 1) if i else u for i in range(8)], axis=1)
                terms = []
                for j in range(taps // 8):
                    moved = pltpu.roll(base, time - 8 * j, 2) if j else base
                    inside = (sample < time - tap_start - 8 * j)[None]
                    terms.append(jnp.where(inside, moved, 0.0))
                stacks.append(jnp.stack(terms, 1).astype(bf16).reshape(sub * taps, time))
            stacked = jnp.concatenate(stacks, axis=1)
            acc_ref[...] += lax.dot_general(
                stacked, k, (((0,), (0,)), ((), ())), preferred_element_type=f32
            )
        return carry

    lax.fori_loop(0, rows // (sub * unroll), body, 0)
    o_ref[...] = acc_ref[...].astype(o_ref.dtype)


def backward(pos, kept, up, before, groups, kind, after):
    _, taps, cols = kept.shape
    rows, width = up.shape
    more = [] if before is None else [before]
    return pl.pallas_call(
        functools.partial(backward_kernel, groups=groups, waits=len(after)),
        in_specs=[SM, ANY, VM] + [ANY] * len(after) + [VM] * len(more),
        out_specs=VM,
        out_shape=jax.ShapeDtypeStruct((width, cols), kind),
        scratch_shapes=[pltpu.VMEM((width, cols), f32)] + ring_of(rows, taps, cols),
        compiler_params=pltpu.CompilerParams(vmem_limit_bytes=40 * MIB),
        cost_estimate=pl.CostEstimate(
            flops=2 * rows * taps * cols * width, bytes_accessed=width * cols * 4, transcendentals=0
        ),
        name="backward",
    )(pos, pltpu.with_memory_space_constraint(kept, pltpu.HBM), up, *after, *more)


def shifted(x, axis, shift):
    n = lax.axis_size(axis)
    return lax.ppermute(x, axis, [(i, (i + shift) % n) for i in range(n)])


def gather(x, axis):
    n = lax.axis_size(axis)
    if n > 8:
        got = lax.all_gather(x, axis)
        return [got[i] for i in range(n)], [jnp.int32(i) for i in range(n)]
    me = lax.axis_index(axis)
    return [x] + [shifted(x, axis, k) for k in range(1, n)], [(me - k) % n for k in range(n)]


def ordered(parts):
    blocks, owners = parts
    if len(blocks) == 2:
        swap = owners[0] > 0
        return [jnp.where(swap, blocks[1], blocks[0]), jnp.where(swap, blocks[0], blocks[1])]
    stack, owners = jnp.stack(blocks), jnp.stack(owners)
    at = jnp.argsort(owners)
    return [lax.dynamic_index_in_dim(stack, at[i], 0, False) for i in range(len(blocks))]


def sum_over(x, axis):
    n = lax.axis_size(axis)
    if n & (n - 1):
        return lax.psum(x, axis)
    step = 1
    while step < n:
        x = x + lax.ppermute(x, axis, [(i, i ^ step) for i in range(n)])
        step *= 2
    return x


def scatter_parts(x, axis):
    n = lax.axis_size(axis)
    me = lax.axis_index(axis)
    if n == 1:
        return [x[0]]
    if n > 8:
        got = lax.all_to_all(x, axis, 0, 0, tiled=True)
        return [got[i] for i in range(n)]
    parts = [lax.dynamic_index_in_dim(x, me, 0, False)]
    for k in range(1, n):
        parts.append(shifted(lax.dynamic_index_in_dim(x, (me + k) % n, 0, False), axis, k))
    return parts


def total_of(parts):
    total = parts[0].astype(f32)
    for part in parts[1:]:
        total = total + part.astype(f32)
    return total


def on_device(response, onset, direct_wave, arrival):
    src_rows, tap_rows, rcv_rows = response.shape
    tile_time = direct_wave.shape[1]
    groups, src_n, tim_n = (lax.axis_size(a) for a in ("grp", "src", "tim"))
    g, s, r, c = (lax.axis_index(a) for a in ("grp", "src", "rcv", "tim"))
    time = src_n * tile_time
    width = groups * time
    rows = src_rows // groups
    part_time = tile_time // tim_n
    halves = 2 if rows % 32 == 0 and rows >= 64 else 1
    half = rows // halves
    share = half // tim_n

    def position(h):
        return jnp.stack([g * rows + h * half, c * tap_rows]).astype(jnp.int32)

    def whole_field(piece):
        if part_time % 16:
            field = piece
            for axis in ("grp", "src", "tim"):
                field = lax.all_gather(field, axis)
            field = field.transpose(2, 1, 0, 3, 4).reshape(1, width, rcv_rows)
            return [field], jnp.zeros((1,), jnp.int32)
        blocks, owners = gather(piece, "grp")
        pair = jnp.stack(blocks)
        where = jnp.stack([o * time for o in owners])
        blocks, owners = gather(pair, "src")
        line = jnp.concatenate(blocks)
        where = jnp.concatenate([where + o * tile_time for o in owners])
        blocks, owners = gather(line, "tim")
        where = jnp.concatenate([where + o * part_time for o in owners])
        return blocks, where.astype(jnp.int32)

    direct_piece = lax.dynamic_slice_in_dim(direct_wave, c * part_time, part_time, 1).T
    my_arrival = lax.dynamic_slice_in_dim(arrival, s * src_rows, src_rows).reshape(groups, rows)
    parts = scatter_parts(my_arrival, "grp")
    owners = [(g - k) % groups if groups <= 8 else jnp.int32(k) for k in range(groups)]
    src_arrival = jnp.stack(ordered((parts, owners)))
    rcv_arrival = lax.dynamic_slice_in_dim(arrival, r * rcv_rows, rcv_rows)

    blocks, where = whole_field(direct_piece)
    kept, energies, energy = [], [], None
    hops = ["tim", "rcv", "grp", "src"]

    def next_energy():
        nonlocal energy
        if not hops:
            return []
        energy = jnp.broadcast_to(sum(energies), (8, 128)) if energy is None else energy
        energy = sum_over(energy, hops.pop(0))
        return [energy]

    up_time = lax.broadcasted_iota(jnp.int32, (1, 1, time), 2)
    piece_time = s * tile_time + c * part_time
    piece_time = piece_time + lax.broadcasted_iota(jnp.int32, (part_time, 1), 0)

    for iteration in range(ITERS):
        final_pass = iteration + 1 == ITERS
        ups, totals, after = [], [], []
        for h in range(halves):
            if iteration == 0:
                partial, muted, squares = first_forward(
                    position(h), where, response, onset, blocks, half, width, after
                )
                kept.append(muted)
                energies.append(squares)
            else:
                partial = forward(position(h), where, kept[h], blocks, width, after)
            partial = partial.astype(bf16).reshape(tim_n, share, width)
            mine = total_of(scatter_parts(partial, "tim")).astype(bf16)
            after = [mine]
            got = gather(mine, "rcv")[0]
            got = got if len(got) == 2 else ordered(gather(mine, "rcv"))
            total = total_of(got).reshape(share, groups, time)
            limit = lax.dynamic_slice_in_dim(src_arrival, h * half + c * share, share, 1)
            total = jnp.where(up_time < limit.T[:, :, None], total, 0.0)
            totals.append(total)
            up = total.reshape(share, width).astype(bf16)
            ups.append(jnp.concatenate(ordered(gather(up, "tim"))))
        acc = None
        for h in range(halves):
            kind = bf16 if h + 1 == halves else f32
            after = (after if h == 0 else []) + next_energy()
            acc = backward(position(h), kept[h], ups[h], acc, groups, kind, after)
        if iteration == 0:
            while hops:
                next_energy()
            unit_gain = lax.rsqrt(energy[0, 0] / STATIONS + 1e-06)
        sums = acc.reshape(groups, src_n, tim_n, part_time, rcv_rows)
        sums = total_of(scatter_parts(sums.transpose(2, 0, 1, 3, 4), "tim")).astype(bf16)
        sums = total_of(scatter_parts(sums, "grp")).astype(bf16)
        sums = total_of(scatter_parts(sums, "src"))
        piece = (
            direct_piece.astype(f32)
            + jnp.where(piece_time < rcv_arrival[None, :], unit_gain * unit_gain * sums, 0.0)
        ).astype(bf16)
        if not final_pass:
            blocks, where = whole_field(piece)
    totals, _ = lax.optimization_barrier((totals, acc))
    out = jnp.stack([(unit_gain * t).astype(bf16) for t in totals])
    out = jnp.stack(ordered(gather(out, "tim")), 1).reshape(rows, groups, time).transpose(1, 0, 2)
    out = scatter_parts(out, "grp")
    focus_up = jnp.concatenate(ordered((out, owners)))
    focus_down = jnp.concatenate(ordered(gather(piece, "tim"))).T
    return (focus_down, focus_up)


def solution(mesh):
    in_specs = (P("src", "tim", "rcv"), P("src", "rcv"), P(("grp", "rcv"), "src"), P("grp"))
    out_specs = (P(("grp", "rcv"), "src"), P(("grp", "src"), None))
    return jax.shard_map(
        on_device, mesh=mesh, in_specs=in_specs, out_specs=out_specs, check_vma=False
    )
```

```python
import functools

import jax
import jax.numpy as jnp
from jax import lax
from jax.experimental import pallas as pl
from jax.experimental.pallas import tpu as pltpu
from jax.sharding import PartitionSpec as P

STATIONS = 2048
ITERS = 2
MIB = 1 << 20
bf16 = jnp.bfloat16
f32 = jnp.float32
VM = pl.BlockSpec(memory_space=pltpu.VMEM)
SM = pl.BlockSpec(memory_space=pltpu.SMEM)
ANY = pl.BlockSpec(memory_space=pl.ANY)


def in_vmem(x):
    return pltpu.with_memory_space_constraint(x, pltpu.VMEM)


def in_hbm(x):
    return pltpu.with_memory_space_constraint(x, pltpu.HBM)


def kept_in(kept):
    if len(kept) == 1:
        return [in_hbm(kept[0])], [ANY]
    return [in_vmem(kept[0]), in_hbm(kept[1])], [VM, ANY]


class Stream:
    def __init__(self, k_hbm, ring, sem, size):
        self.k_hbm, self.ring, self.sem, self.size = k_hbm, ring, sem, size
        self.slots, self.count = ring.shape[0], k_hbm.shape[0] // size

    def copy(self, step):
        slot = lax.rem(step, self.slots)
        return pltpu.make_async_copy(
            self.k_hbm.at[pl.ds(step * self.size, self.size)], self.ring.at[slot], self.sem.at[slot]
        )

    def start(self):
        for c in range(min(self.slots - 1, self.count)):
            self.copy(jnp.int32(c)).start()

    def next(self, step):
        self.copy(step).wait()

        @pl.when(step + self.slots - 1 < self.count)
        def _():
            self.copy(step + self.slots - 1).start()

        return lax.rem(step, self.slots)


def ring_of(rows, taps, cols):
    sub, unroll = steps_of(rows)
    return [pltpu.VMEM((3, sub * unroll, taps, cols), bf16), pltpu.SemaphoreType.DMA((3,))]


def steps_of(rows):
    sub = 16 if rows >= 32 else rows // 2
    unroll = 2 if rows % (2 * sub) == 0 and rows > 2 * sub else 1
    return sub, unroll


def place_blocks(where_ref, blocks, f_ref):
    many, size = blocks[0].shape[0], blocks[0].shape[1]
    for b, block in enumerate(blocks):
        for i in range(many):
            to = where_ref[b * many + i]
            f_ref[pl.ds(pl.multiple_of(to, size), size)] = block[i]


def shear_sum(k, f_ref, tap_start, groups, put):
    sub, taps, cols = k.shape
    time = f_ref.shape[0] // groups
    sample = lax.broadcasted_iota(jnp.int32, (8, time), 0) + lax.broadcasted_iota(
        jnp.int32, (8, time), 1
    )
    p = lax.dot_general(
        k.reshape(sub * taps, cols),
        f_ref[...],
        (((1,), (1,)), ((), ())),
        preferred_element_type=f32,
    )
    p = p.reshape(sub, taps // 8, 8, groups * time)
    for g in range(groups):
        total = None
        for j in range(taps // 8 - 1, -1, -1):
            inside = (sample < time - tap_start - 8 * j)[None]
            term = jnp.where(inside, p[:, j, :, g * time : (g + 1) * time], 0.0)
            total = term if total is None else pltpu.roll(total, 8, 2) + term
        total = pltpu.roll(total, 0, 2, stride=1, stride_axis=1)
        put(g * time, (g + 1) * time, pltpu.roll(jnp.sum(total, axis=1), tap_start, 1))


def forward_kernel(pos_ref, where_ref, *refs, groups, waits, near):
    head_ref, k_hbm, refs = refs[0], refs[near], refs[1 + near :]
    blocks, (o_ref, f_ref, ring, sem) = refs[waits:-4], refs[-4:]
    rows = o_ref.shape[0]
    sub, unroll = steps_of(rows)
    stream = Stream(k_hbm, ring, sem, sub * unroll)
    stream.start()
    tap_start = pos_ref[1]
    place_blocks(where_ref, blocks, f_ref)

    def work(step, now_ref):
        for u in range(unroll):
            at = pl.multiple_of((step * unroll + u) * sub, sub)

            def put(lo, hi, value):
                o_ref[pl.ds(at, sub), lo:hi] = value

            k = now_ref[u * sub : (u + 1) * sub]
            shear_sum(k, f_ref, tap_start, groups, put)

    def body(step, carry):
        work(step, ring.at[stream.next(step - near)])
        return carry

    if near:
        work(0, head_ref)
    lax.fori_loop(near, rows // (sub * unroll), body, 0)


def first_kernel(pos_ref, where_ref, r_hbm, on_hbm, *refs, groups, waits, near):
    blocks, refs = refs[waits : -10 - near], refs[-10 - near :]
    head_hbm, refs = refs[1], refs[:1] + refs[1 + near :]
    o_ref, k_hbm, e_out, f_ref, ring, sem, out_sem, on_ref, e_ref, on_sem = refs
    rows = o_ref.shape[0]
    _, taps, cols = k_hbm.shape
    sub, unroll = steps_of(rows)
    size, slots = sub * unroll, ring.shape[0]
    count = rows // size
    ahead = slots - 2
    start = pl.multiple_of(pos_ref[0], 8)
    tap_start = pos_ref[1]

    def part(step):
        slot = lax.rem(step, slots)
        return pltpu.make_async_copy(
            r_hbm.at[pl.ds(start + step * size, size)], ring.at[slot], sem.at[slot]
        )

    def result(step):
        slot = lax.rem(step, slots)
        at = jnp.maximum(step - near, 0) * size
        return pltpu.make_async_copy(ring.at[slot], k_hbm.at[pl.ds(at, size)], out_sem.at[slot])

    onset_copy = pltpu.make_async_copy(on_hbm.at[pl.ds(start, rows)], on_ref, on_sem)
    onset_copy.start()
    for n in range(min(ahead, count)):
        part(jnp.int32(n)).start()
    e_ref[...] = jnp.zeros_like(e_ref)
    tap = lax.broadcasted_iota(jnp.int32, (1, taps, 1), 1).astype(f32).astype(bf16)
    place_blocks(where_ref, blocks, f_ref)
    onset_copy.wait()

    def body(step, carry):
        slot = lax.rem(step, slots)
        part(step).wait()

        @pl.when(step + ahead < count)
        def _():
            @pl.when(step >= slots - ahead)
            def _():
                result(step - (slots - ahead)).wait()

            part(step + ahead).start()

        for u in range(unroll):
            at = pl.multiple_of((step * unroll + u) * sub, sub)

            def put(lo, hi, value):
                o_ref[pl.ds(at, sub), lo:hi] = value

            for v in range(0, sub, 8):
                r = ring[slot, u * sub + v : u * sub + v + 8]
                x = r.astype(f32)
                e_ref[...] += jnp.sum((x * x).reshape(taps, 8, cols), axis=0)
                on = (on_ref[pl.ds(at + v, 8)] - tap_start).astype(f32).astype(bf16)
                keep = jnp.broadcast_to(tap, r.shape) >= on[:, None, :]
                ring[slot, u * sub + v : u * sub + v + 8] = jnp.where(keep, r, jnp.zeros((), bf16))
            k = ring[slot, u * sub : (u + 1) * sub]
            shear_sum(k, f_ref, tap_start, groups, put)
        if near:

            @pl.when(step == 0)
            def _():
                pltpu.make_async_copy(ring.at[slot], head_hbm, out_sem.at[slot]).start()

        @pl.when(step >= near)
        def _():
            result(step).start()

        return carry

    lax.fori_loop(0, count, body, 0)
    for n in range(max(0, count - slots), count):
        result(jnp.int32(n)).wait()
    e_out[0] = jnp.sum(e_ref[...])


def first_forward(pos, where, response, onset, blocks, rows, width, after, near):
    _, taps, cols = response.shape
    groups = lax.axis_size("grp")
    sub, unroll = steps_of(rows)
    parts = [sub * unroll, rows - sub * unroll] if near else [rows]
    kept = [pltpu.HBM((n, taps, cols), bf16) for n in parts]
    slots = 4
    return pl.pallas_call(
        functools.partial(first_kernel, groups=groups, waits=len(after), near=near),
        in_specs=[SM, SM, ANY, ANY] + [ANY] * len(after) + [VM] * len(blocks),
        out_specs=[VM] + [ANY] * len(kept) + [SM],
        out_shape=[
            jax.ShapeDtypeStruct((rows, width), f32),
            *kept,
            jax.ShapeDtypeStruct((1,), f32),
        ],
        scratch_shapes=[
            pltpu.VMEM((width, cols), bf16),
            pltpu.VMEM((slots, sub * unroll, taps, cols), bf16),
            pltpu.SemaphoreType.DMA((slots,)),
            pltpu.SemaphoreType.DMA((slots,)),
            pltpu.VMEM((rows, cols), jnp.int32),
            pltpu.VMEM((8, cols), f32),
            pltpu.SemaphoreType.DMA,
        ],
        compiler_params=pltpu.CompilerParams(vmem_limit_bytes=44 * MIB),
        cost_estimate=pl.CostEstimate(
            flops=2 * rows * taps * cols * width, bytes_accessed=width * cols * 2, transcendentals=0
        ),
        name="first_forward",
    )(pos, where, response, onset, *after, *blocks)


def forward(pos, where, kept, blocks, width, after):
    muted, places = kept_in(kept)
    near = len(muted) - 1
    _, taps, cols = kept[0].shape
    rows = sum(k.shape[0] for k in kept)
    groups = lax.axis_size("grp")
    return pl.pallas_call(
        functools.partial(forward_kernel, groups=groups, waits=len(after), near=near),
        in_specs=[SM, SM] + places + [ANY] * len(after) + [VM] * len(blocks),
        out_specs=VM,
        out_shape=jax.ShapeDtypeStruct((rows, width), f32),
        scratch_shapes=[pltpu.VMEM((width, cols), bf16)] + ring_of(rows, taps, cols),
        compiler_params=pltpu.CompilerParams(vmem_limit_bytes=32 * MIB),
        cost_estimate=pl.CostEstimate(
            flops=2 * rows * taps * cols * width, bytes_accessed=width * cols * 2, transcendentals=0
        ),
        name="forward",
    )(pos, where, *muted, *after, *blocks)


def backward_kernel(pos_ref, *refs, groups, waits, near):
    head_ref, k_hbm, u_ref, refs = refs[0], refs[near], refs[1 + near], refs[2 + near + waits :]
    before_ref, (o_ref, acc_ref, ring, sem) = (refs[0] if len(refs) == 5 else None), refs[-4:]
    _, taps, cols = k_hbm.shape
    rows = u_ref.shape[0]
    sub, unroll = steps_of(rows)
    stream = Stream(k_hbm, ring, sem, sub * unroll)
    stream.start()
    time = u_ref.shape[1] // groups
    tap_start = pos_ref[1]
    sample = lax.broadcasted_iota(jnp.int32, (8, time), 0) + lax.broadcasted_iota(
        jnp.int32, (8, time), 1
    )
    acc_ref[...] = jnp.zeros_like(acc_ref) if before_ref is None else before_ref[...]

    def work(step, now_ref):
        for n in range(unroll):
            at = pl.multiple_of((step * unroll + n) * sub, sub)
            k = now_ref[n * sub : (n + 1) * sub].reshape(sub * taps, cols)
            stacks = []
            for g in range(groups):
                u = u_ref[pl.ds(at, sub), g * time : (g + 1) * time].astype(f32)
                u = pltpu.roll(u, time - tap_start, 1)
                base = jnp.stack([pltpu.roll(u, time - i, 1) if i else u for i in range(8)], axis=1)
                terms = []
                for j in range(taps // 8):
                    moved = pltpu.roll(base, time - 8 * j, 2) if j else base
                    inside = (sample < time - tap_start - 8 * j)[None]
                    terms.append(jnp.where(inside, moved, 0.0))
                stacks.append(jnp.stack(terms, 1).astype(bf16).reshape(sub * taps, time))
            stacked = jnp.concatenate(stacks, axis=1)
            acc_ref[...] += lax.dot_general(
                stacked, k, (((0,), (0,)), ((), ())), preferred_element_type=f32
            )

    def body(step, carry):
        work(step, ring.at[stream.next(step - near)])
        return carry

    if near:
        work(0, head_ref)
    lax.fori_loop(near, rows // (sub * unroll), body, 0)
    o_ref[...] = acc_ref[...].astype(o_ref.dtype)


def backward(pos, kept, up, before, groups, kind, after):
    muted, places = kept_in(kept)
    near = len(muted) - 1
    _, taps, cols = kept[0].shape
    rows, width = up.shape
    more = [] if before is None else [before]
    return pl.pallas_call(
        functools.partial(backward_kernel, groups=groups, waits=len(after), near=near),
        in_specs=[SM] + places + [VM] + [ANY] * len(after) + [VM] * len(more),
        out_specs=VM,
        out_shape=jax.ShapeDtypeStruct((width, cols), kind),
        scratch_shapes=[pltpu.VMEM((width, cols), f32)] + ring_of(rows, taps, cols),
        compiler_params=pltpu.CompilerParams(vmem_limit_bytes=32 * MIB),
        cost_estimate=pl.CostEstimate(
            flops=2 * rows * taps * cols * width, bytes_accessed=width * cols * 4, transcendentals=0
        ),
        name="backward",
    )(pos, *muted, up, *after, *more)


def shifted(x, axis, shift):
    n = lax.axis_size(axis)
    return lax.ppermute(x, axis, [(i, (i + shift) % n) for i in range(n)])


def gather(x, axis):
    n = lax.axis_size(axis)
    if n > 8:
        got = lax.all_gather(x, axis)
        return [got[i] for i in range(n)], [jnp.int32(i) for i in range(n)]
    me = lax.axis_index(axis)
    return [x] + [shifted(x, axis, k) for k in range(1, n)], [(me - k) % n for k in range(n)]


def ordered(parts):
    blocks, owners = parts
    if len(blocks) == 2:
        swap = owners[0] > 0
        return [jnp.where(swap, blocks[1], blocks[0]), jnp.where(swap, blocks[0], blocks[1])]
    stack, owners = jnp.stack(blocks), jnp.stack(owners)
    at = jnp.argsort(owners)
    return [lax.dynamic_index_in_dim(stack, at[i], 0, False) for i in range(len(blocks))]


def sum_over(x, axes):
    n = 1
    for axis in axes:
        n *= lax.axis_size(axis)

    def from_other(x, step):
        return lax.ppermute(x, axes, [(i, i ^ step) for i in range(n)])

    if n & (n - 1):
        return lax.psum(x, axes)
    if n == 4:
        return (x + from_other(x, 1)) + (from_other(x, 2) + from_other(x, 3))
    step = 1
    while step < n:
        x = x + from_other(x, step)
        step *= 2
    return x


def scatter_parts(x, axis):
    n = lax.axis_size(axis)
    me = lax.axis_index(axis)
    if n == 1:
        return [x[0]]
    if n > 8:
        got = lax.all_to_all(x, axis, 0, 0, tiled=True)
        return [got[i] for i in range(n)]
    parts = [lax.dynamic_index_in_dim(x, me, 0, False)]
    for k in range(1, n):
        parts.append(shifted(lax.dynamic_index_in_dim(x, (me + k) % n, 0, False), axis, k))
    return parts


def total_of(parts):
    total = parts[0].astype(f32)
    for part in parts[1:]:
        total = total + part.astype(f32)
    return total


def on_device(response, onset, direct_wave, arrival):
    src_rows, tap_rows, rcv_rows = response.shape
    tile_time = direct_wave.shape[1]
    groups, src_n, tim_n = (lax.axis_size(a) for a in ("grp", "src", "tim"))
    g, s, r, c = (lax.axis_index(a) for a in ("grp", "src", "rcv", "tim"))
    time = src_n * tile_time
    width = groups * time
    rows = src_rows // groups
    part_time = tile_time // tim_n
    halves = 2 if rows % 32 == 0 and rows >= 64 else 1
    half = rows // halves
    share = half // tim_n

    def position(h):
        return jnp.stack([g * rows + h * half, c * tap_rows]).astype(jnp.int32)

    def whole_field(piece):
        if part_time % 16:
            field = piece
            for axis in ("grp", "src", "tim"):
                field = lax.all_gather(field, axis)
            field = field.transpose(2, 1, 0, 3, 4).reshape(1, width, rcv_rows)
            return [field], jnp.zeros((1,), jnp.int32)
        blocks, owners = gather(piece, "grp")
        pair = jnp.stack(blocks)
        where = jnp.stack([o * time for o in owners])
        blocks, owners = gather(pair, "src")
        line = jnp.concatenate(blocks)
        where = jnp.concatenate([where + o * tile_time for o in owners])
        blocks, owners = gather(line, "tim")
        where = jnp.concatenate([where + o * part_time for o in owners])
        return blocks, where.astype(jnp.int32)

    direct_piece = lax.dynamic_slice_in_dim(direct_wave, c * part_time, part_time, 1).T
    my_arrival = lax.dynamic_slice_in_dim(arrival, s * src_rows, src_rows).reshape(groups, rows)
    parts = scatter_parts(my_arrival, "grp")
    owners = [(g - k) % groups if groups <= 8 else jnp.int32(k) for k in range(groups)]
    src_arrival = jnp.stack(ordered((parts, owners)))
    rcv_arrival = lax.dynamic_slice_in_dim(arrival, r * rcv_rows, rcv_rows)

    blocks, where = whole_field(direct_piece)
    kept, energies, energy = [], [], None
    hops = [("tim",), ("grp", "rcv"), ("src",)]

    def next_energy():
        nonlocal energy
        if not hops:
            return []
        energy = jnp.broadcast_to(sum(energies), (8, 128)) if energy is None else energy
        energy = sum_over(energy, hops.pop(0))
        return [energy]

    up_time = lax.broadcasted_iota(jnp.int32, (1, 1, time), 2)
    piece_time = s * tile_time + c * part_time
    piece_time = piece_time + lax.broadcasted_iota(jnp.int32, (part_time, 1), 0)

    for iteration in range(ITERS):
        final_pass = iteration + 1 == ITERS
        ups, totals, after = [], [], []
        for h in range(halves):
            if iteration == 0:
                partial, *muted, squares = first_forward(
                    position(h), where, response, onset, blocks, half, width, after, min(h, 1)
                )
                kept.append(muted)
                energies.append(squares)
            else:
                partial = forward(position(h), where, kept[h], blocks, width, after)
            partial = partial.astype(bf16).reshape(tim_n, share, width)
            mine = total_of(scatter_parts(partial, "tim")).astype(bf16)
            after = [mine]
            got = gather(mine, "rcv")[0]
            got = got if len(got) == 2 else ordered(gather(mine, "rcv"))
            total = total_of(got).reshape(share, groups, time)
            limit = lax.dynamic_slice_in_dim(src_arrival, h * half + c * share, share, 1)
            total = jnp.where(up_time < limit.T[:, :, None], total, 0.0)
            totals.append(total)
            up = total.reshape(share, width).astype(bf16)
            ups.append(jnp.concatenate(ordered(gather(up, "tim"))))
        acc = None
        for h in range(halves):
            kind = bf16 if h + 1 == halves else f32
            after = (after if h == 0 else []) + next_energy()
            acc = backward(position(h), kept[h], ups[h], acc, groups, kind, after)
        if iteration == 0:
            while hops:
                next_energy()
            unit_gain = lax.rsqrt(energy[0, 0] / STATIONS + 1e-06)
        sums = acc.reshape(groups, src_n, tim_n, part_time, rcv_rows)
        sums = total_of(scatter_parts(sums.transpose(2, 0, 1, 3, 4), "tim")).astype(bf16)
        sums = total_of(scatter_parts(sums, "grp")).astype(bf16)
        sums = total_of(scatter_parts(sums, "src"))
        piece = (
            direct_piece.astype(f32)
            + jnp.where(piece_time < rcv_arrival[None, :], unit_gain * unit_gain * sums, 0.0)
        ).astype(bf16)
        if not final_pass:
            blocks, where = whole_field(piece)
    totals, _ = lax.optimization_barrier((totals, acc))
    out = jnp.stack([(unit_gain * t).astype(bf16) for t in totals])
    out = jnp.stack(ordered(gather(out, "tim")), 1).reshape(rows, groups, time).transpose(1, 0, 2)
    out = scatter_parts(out, "grp")
    focus_up = jnp.concatenate(ordered((out, owners)))
    focus_down = jnp.concatenate(ordered(gather(piece, "tim"))).T
    return (focus_down, focus_up)


def solution(mesh):
    in_specs = (P("src", "tim", "rcv"), P("src", "rcv"), P(("grp", "rcv"), "src"), P("grp"))
    out_specs = (P(("grp", "rcv"), "src"), P(("grp", "src"), None))
    return jax.shard_map(
        on_device, mesh=mesh, in_specs=in_specs, out_specs=out_specs, check_vma=False
    )
```
